256 devices in a mesh: tm: 32 (over z, x_hi, core), gz: 8 (over x_lo, y).
Axes of the slice: x: 4 (x_hi: 2, x_lo: 2; x = x_hi * 2 + x_lo), y: 4, z: 8, core: 2. Of those that a mesh axis runs over, the one named last changes fastest.
Arguments:
- starts: float32 [32, 32, 32, 128], P('tm', 'gz'), may hold values from -6 to 6
- cell_rates: float32 [32, 32, 128], P('gz'), may hold values from 0.3 to 1
Outputs:
- slab_ends: float32 [32, 32, 32, 128], P('tm', 'gz')
- next_starts: float32 [32, 32, 32, 128], P('tm', 'gz')
The draws below stay inside these ranges and needn't reach their ends.
All inputs are finite; a program needn't handle non-finite values.
Results may differ from the reference program's by a relative error of at most 0.0001.
Values sent between devices are 32-bit elements; how exact they have to be, the bound alone decides.
No kernel may reach another device: no remote copies, remote signals or barrier semaphores. Data moves between devices by JAX's collectives and lax.ppermute only.
A program may use at most 64 MiB of HBM per device.

```python
import jax
import jax.numpy as jnp
from jax import lax

NX = 32
NY = 128
FINE = 4
SLABS = 32
NZ = 32


def draw_starts(key, part):
    rough = jnp.clip(jax.random.normal(key, (SLABS, NZ, NX, NY), jnp.float32), -6.0, 6.0)
    return rough


def block_levels(own_key, extent, pieces, low, largest):
    def one(position, blocks):
        draws = jax.random.uniform(jax.random.fold_in(jax.random.fold_in(own_key, 6), position), (blocks,), jnp.float32, low / len(pieces), largest / len(pieces))
        return jnp.repeat(jnp.exp(draws), extent[position] // blocks).reshape((-1,) + (1,) * (len(extent) - position - 1))

    factor_of = one(*pieces[0])
    for cut in pieces[1:]:
        factor_of = factor_of * one(*cut)
    return factor_of


def setup_inputs(seed: int = 0) -> dict:
    keys = jax.random.split(jax.random.key(seed), 3)
    starts = draw_starts(jax.random.fold_in(keys[2], 71), 0)
    cell_rates = jnp.clip(0.3 + 0.7 * jax.random.uniform(keys[1], (NZ, NX, NY), jnp.float32) ** block_levels(keys[1], (NZ, NX, NY), ((0, 8),), -0.2, 0.2), 0.3, 1.0)
    return dict(starts=starts, cell_rates=cell_rates)


fine_along_z = (0.1, 0.12)
fine_along_x = (0.15, 0.12)
fine_along_y = (0.2, 0.12)
coarse_along_z = (0.2, 0.25)
coarse_along_x = (0.3, 0.25)
coarse_along_y = (0.4, 0.25)


def line_filter(behind, middle, beyond, courant, diffuse):
    return (diffuse + 0.5 * courant) * behind + (1.0 - 2.0 * diffuse) * middle + (diffuse - 0.5 * courant) * beyond


def smooth_step(values, weights, along_z, along_x, along_y):
    mixed = line_filter(jnp.roll(values, 1, 2), values, jnp.roll(values, -1, 2), along_y[0], along_y[1])
    mixed = line_filter(jnp.roll(mixed, 1, 1), mixed, jnp.roll(mixed, -1, 1), along_x[0], along_x[1])
    mixed = line_filter(jnp.roll(mixed, 1, 0), mixed, jnp.roll(mixed, -1, 0), along_z[0], along_z[1])
    return values + weights * (mixed - values)


def restrict(values):
    extent_z, extent_x, extent_y = values.shape
    blocks = values.reshape(extent_z // 2, 2, extent_x // 2, 2, extent_y // 2, 2)
    return jnp.mean(blocks, axis=(1, 3, 5))


def prolong(values):
    extent_z, extent_x, extent_y = values.shape
    spread = jnp.broadcast_to(values[:, None, :, None, :, None], (extent_z, 2, extent_x, 2, extent_y, 2))
    return spread.reshape(extent_z * 2, extent_x * 2, extent_y * 2)


def propagate(values, coarse_rates):
    coarse = smooth_step(restrict(values), coarse_rates, coarse_along_z, coarse_along_x, coarse_along_y)
    return prolong(coarse)


def fine_solve(values, cell_rates):
    for sweep_index in range(FINE):
        values = smooth_step(values, cell_rates, fine_along_z, fine_along_x, fine_along_y)
    return values


def reference(starts, cell_rates):
    coarse_rates = restrict(cell_rates)

    def slab_correction(start):
        return fine_solve(start, cell_rates) - propagate(start, coarse_rates)

    correction = lax.map(slab_correction, starts)

    def link(current, term):
        finish = propagate(current, coarse_rates) + term
        return finish, finish

    _, slab_ends = lax.scan(link, starts[0], correction)
    next_starts = jnp.concatenate([slab_ends[-1:], slab_ends[:-1]], axis=0)
    return slab_ends, next_starts
```

```python
import jax
import jax.numpy as jnp
from jax import lax
from jax.experimental import pallas as pl
from jax.experimental.pallas import tpu as pltpu
from jax.sharding import Mesh, PartitionSpec as P

FINE = 4
STEPS = 32
GROUP = 4

fine_along_z = (0.1, 0.12)
fine_along_x = (0.15, 0.12)
fine_along_y = (0.2, 0.12)
coarse_along_z = (0.2, 0.25)
coarse_along_x = (0.3, 0.25)
coarse_along_y = (0.4, 0.25)

AXES = ("z", "h", "c", "l", "y")
SLAB = ("z", "h", "c")
GRID = ("l", "y")
PLANE = ("h", "c", "l", "y")


def weights_of(kind):
    courant, diffuse = kind
    return diffuse + 0.5 * courant, 1.0 - 2.0 * diffuse, diffuse - 0.5 * courant


def line_filter(behind, middle, beyond, kind):
    a, b, c = weights_of(kind)
    return a * behind + b * middle + c * beyond


def even_lanes():
    return lax.broadcasted_iota(jnp.int32, (8, 128), 1) % 2 == 0


def packed_plane_filter(v, even):
    v = line_filter(pltpu.roll(v, 2, 1), v, pltpu.roll(v, 126, 1), coarse_along_y)
    right, left = pltpu.roll(v, 1, 1), pltpu.roll(v, 127, 1)
    behind = jnp.where(even, pltpu.roll(left, 1, 0), right)
    beyond = jnp.where(even, left, pltpu.roll(right, 7, 0))
    return line_filter(behind, v, beyond, coarse_along_x)


def packed_layer(ref, first, even):
    def rows(at):
        near = ref[pl.ds(first + at, 8, stride=4), :] + ref[pl.ds(first + at + 1, 8, stride=4), :]
        far = ref[pl.ds(first + 32 + at, 8, stride=4), :] + ref[pl.ds(first + 33 + at, 8, stride=4), :]
        return near + far

    low, high = rows(0), rows(2)
    return 0.125 * jnp.where(even, low + pltpu.roll(low, 127, 1), high + pltpu.roll(high, 1, 1))


def fine_kernel(start, rates, low, high, smooth_out, send_out, wide, ends):
    even = even_lanes()
    is_first = (lax.axis_index("z") == 0) & (lax.axis_index("h") == 0) & (lax.axis_index("c") == 0)
    wide[0:128] = low[0:128]
    wide[128:256] = start[...]
    wide[256:384] = high[0:128]
    current = wide[...].reshape(12, 32, 128)
    rate = jnp.concatenate([low[128:256], rates[...], high[128:256]], axis=0).reshape(12, 32, 128)
    for _ in range(FINE):
        mixed = line_filter(
            pltpu.roll(current, 1, 2), current, pltpu.roll(current, 127, 2), fine_along_y
        )
        mixed = line_filter(pltpu.roll(mixed, 1, 1), mixed, pltpu.roll(mixed, 31, 1), fine_along_x)
        mixed = line_filter(mixed[:-2], mixed[1:-1], mixed[2:], fine_along_z)
        current, rate = current[1:-1], rate[1:-1]
        current = current + rate * (mixed - current)
    ends[...] = current.reshape(128, 128)
    coarse = [packed_layer(wide, 64 + 64 * i, even) for i in range(4)]
    flat = [packed_plane_filter(v, even) for v in coarse]
    coarse_rates, terms = [], []
    for i in range(2):
        coarse_rates.append(packed_layer(rates, 64 * i, even))
        mixed = line_filter(flat[i], flat[i + 1], flat[i + 2], coarse_along_z)
        guess = coarse[i + 1] + coarse_rates[i] * (mixed - coarse[i + 1])
        end = packed_layer(ends, 64 * i, even)
        terms.append(end - jnp.where(is_first, jnp.zeros_like(guess), guess))
        add_spread(smooth_out, ends, 64 * i, -end, even)
    own = jnp.where(lax.axis_index("h") == 0, coarse_rates[0], coarse_rates[1])
    message = jnp.concatenate([*terms, own], axis=0)
    send_out[...] = jnp.broadcast_to(message[None], send_out.shape)


def chain_kernel(received, send_out, history):
    even = even_lanes()
    depth = range(16)
    rates = [received[16 * (z % 2) + z // 2, 16:24] for z in depth]

    def term(step):
        return [received[8 * step + z // 2, 8 * (z % 2) : 8 * (z % 2) + 8] for z in depth]

    def keep(step, layers):
        for z in depth:
            history[step, z] = layers[z]

    def advance(layers):
        flat = [packed_plane_filter(v, even) for v in layers]
        out = []
        for z in depth:
            mixed = line_filter(flat[z - 1], flat[z], flat[(z + 1) % 16], coarse_along_z)
            out.append(layers[z] + rates[z] * (mixed - layers[z]))
        return out

    history[0] = jnp.zeros((16, 8, 128), jnp.float32)
    layers = term(0)
    keep(1, layers)
    for step in range(1, GROUP):
        layers = [a + b for a, b in zip(advance(layers), term(step))]
        keep(step + 1, layers)

    def body(step, layers):
        layers = advance(layers)
        keep(step + 1, layers)
        return tuple(layers)

    lax.fori_loop(GROUP, STEPS, body, tuple(layers))
    mine = lax.axis_index("z")
    place = lax.axis_index("h") * 2 + lax.axis_index("c")
    first = (lax.axis_index("l") * 4 + lax.axis_index("y")) * 2
    for target in range(8):
        begin = jnp.where(mine <= target, GROUP * (target - mine) + place, 0)
        finish = jnp.where(mine <= target, GROUP * (target - mine) + place + 1, 0)
        if target == 0:
            begin = jnp.where(place == 0, STEPS - GROUP * mine, begin)
        send_out[target, 0:16] = history[begin, pl.ds(first, 2)].reshape(16, 128)
        send_out[target, 16:32] = history[finish, pl.ds(first, 2)].reshape(16, 128)


def add_spread(out, smooth, first, layer, even):
    low = jnp.where(even, layer, pltpu.roll(layer, 1, 1))
    high = jnp.where(even, pltpu.roll(layer, 127, 1), layer)
    for plane in (0, 32):
        for at, value in ((0, low), (1, low), (2, high), (3, high)):
            rows = pl.ds(first + plane + at, 8, stride=4)
            out[rows, :] = smooth[rows, :] + value


def finish_kernel(received, smooth, smooth_before, ends_out, starts_out):
    even = even_lanes()
    total = received[0]
    for source in range(1, 8):
        total = total + received[source]
    for i in range(2):
        add_spread(starts_out, smooth_before, 64 * i, total[8 * i : 8 * i + 8], even)
        add_spread(ends_out, smooth, 64 * i, total[16 + 8 * i : 24 + 8 * i], even)


def array(*shape):
    return jax.ShapeDtypeStruct(shape, jnp.float32)


def cost(operations, size):
    return pl.CostEstimate(flops=operations, bytes_accessed=size, transcendentals=0)


def per_device(starts, cell_rates):
    start = starts.reshape(128, 128)
    rates = cell_rates.reshape(128, 128)
    both = jnp.concatenate([start, rates], axis=0)
    low = lax.ppermute(both, GRID, [(i, (i + 1) % 8) for i in range(8)])
    high = lax.ppermute(both, GRID, [((i + 1) % 8, i) for i in range(8)])
    smooth, message = pl.pallas_call(
        fine_kernel,
        out_shape=(array(128, 128), array(32, 24, 128)),
        scratch_shapes=[pltpu.VMEM((384, 128), jnp.float32), pltpu.VMEM((128, 128), jnp.float32)],
        cost_estimate=cost(4_000_000, 800_000),
        name="fine",
    )(start, rates, low, high)
    gathered = lax.all_to_all(message, PLANE, 0, 0, tiled=True)
    smooth_before = lax.ppermute(smooth, SLAB, [(i, (i + 1) % 32) for i in range(32)])
    pieces = pl.pallas_call(
        chain_kernel,
        out_shape=array(8, 32, 128),
        scratch_shapes=[pltpu.VMEM((STEPS + 1, 16, 8, 128), jnp.float32)],
        cost_estimate=cost(12_000_000, 500_000),
        name="chain",
    )(gathered)
    shares = lax.all_to_all(pieces, ("z",), 0, 0, tiled=True)
    ends, nexts = pl.pallas_call(
        finish_kernel,
        out_shape=(array(128, 128), array(128, 128)),
        cost_estimate=cost(200_000, 400_000),
        name="finish",
    )(shares, smooth, smooth_before)
    return ends.reshape(1, 4, 32, 128), nexts.reshape(1, 4, 32, 128)


def solution(mesh):
    fine_mesh = Mesh(mesh.devices.reshape(8, 2, 2, 2, 4), AXES)
    state = P(SLAB, GRID, None, None)
    return jax.shard_map(
        per_device,
        mesh=fine_mesh,
        in_specs=(state, P(GRID, None, None)),
        out_specs=(state, state),
        check_vma=False,
    )
```

```python
import jax
import jax.numpy as jnp
from jax import lax
from jax.experimental import pallas as pl
from jax.experimental.pallas import tpu as pltpu
from jax.sharding import Mesh, PartitionSpec as P

FINE = 4
STEPS = 32
GROUP = 4

fine_along_z = (0.1, 0.12)
fine_along_x = (0.15, 0.12)
fine_along_y = (0.2, 0.12)
coarse_along_z = (0.2, 0.25)
coarse_along_x = (0.3, 0.25)
coarse_along_y = (0.4, 0.25)

AXES = ("z", "h", "c", "l", "y")
SLAB = ("z", "h", "c")
GRID = ("l", "y")
PLANE = ("h", "c", "l", "y")


def weights_of(kind):
    courant, diffuse = kind
    return diffuse + 0.5 * courant, 1.0 - 2.0 * diffuse, diffuse - 0.5 * courant


def line_filter(behind, middle, beyond, kind):
    a, b, c = weights_of(kind)
    return a * behind + b * middle + c * beyond


def even_lanes():
    return lax.broadcasted_iota(jnp.int32, (8, 128), 1) % 2 == 0


def packed_plane_filter(v, even):
    v = line_filter(pltpu.roll(v, 2, 1), v, pltpu.roll(v, 126, 1), coarse_along_y)
    right, left = pltpu.roll(v, 1, 1), pltpu.roll(v, 127, 1)
    behind = jnp.where(even, pltpu.roll(left, 1, 0), right)
    beyond = jnp.where(even, left, pltpu.roll(right, 7, 0))
    return line_filter(behind, v, beyond, coarse_along_x)


def packed_layer(ref, first, even):
    def rows(at):
        near = ref[pl.ds(first + at, 8, stride=4), :] + ref[pl.ds(first + at + 1, 8, stride=4), :]
        far = ref[pl.ds(first + 32 + at, 8, stride=4), :] + ref[pl.ds(first + 33 + at, 8, stride=4), :]
        return near + far

    low, high = rows(0), rows(2)
    return 0.125 * jnp.where(even, low + pltpu.roll(low, 127, 1), high + pltpu.roll(high, 1, 1))


def fine_kernel(own, low, high, smooth_out, send_out, wide, ends, rates):
    even = even_lanes()
    is_first = (lax.axis_index("z") == 0) & (lax.axis_index("h") == 0) & (lax.axis_index("c") == 0)
    wide[0:128] = low[0:128]
    wide[128:256] = own[0:128]
    rates[...] = own[128:256]
    wide[256:384] = high[0:128]
    current = wide[...].reshape(12, 32, 128)
    rate = jnp.concatenate([low[128:256], rates[...], high[128:256]], axis=0).reshape(12, 32, 128)
    for _ in range(FINE):
        mixed = line_filter(
            pltpu.roll(current, 1, 2), current, pltpu.roll(current, 127, 2), fine_along_y
        )
        mixed = line_filter(pltpu.roll(mixed, 1, 1), mixed, pltpu.roll(mixed, 31, 1), fine_along_x)
        mixed = line_filter(mixed[:-2], mixed[1:-1], mixed[2:], fine_along_z)
        current, rate = current[1:-1], rate[1:-1]
        current = current + rate * (mixed - current)
    ends[...] = current.reshape(128, 128)
    coarse = [packed_layer(wide, 64 + 64 * i, even) for i in range(4)]
    flat = [packed_plane_filter(v, even) for v in coarse]
    coarse_rates, terms = [], []
    for i in range(2):
        coarse_rates.append(packed_layer(rates, 64 * i, even))
        mixed = line_filter(flat[i], flat[i + 1], flat[i + 2], coarse_along_z)
        guess = coarse[i + 1] + coarse_rates[i] * (mixed - coarse[i + 1])
        end = packed_layer(ends, 64 * i, even)
        terms.append(end - jnp.where(is_first, jnp.zeros_like(guess), guess))
        add_spread(smooth_out, ends, 64 * i, -end, even)
    layer = jnp.where(lax.axis_index("h") == 0, coarse_rates[0], coarse_rates[1])
    message = jnp.concatenate([*terms, layer], axis=0)
    send_out[...] = jnp.broadcast_to(message[None], send_out.shape)


def side_weights(kind):
    a, b, c = weights_of(kind)
    return a / b, c / b


def scaled_filter(behind, middle, beyond, kind):
    a, c = side_weights(kind)
    return middle + (a * behind + c * beyond)


def scaled_plane_filter(v, even):
    near, far = {}, {}
    for by in (1, 2, 3):
        near[by], far[by] = pltpu.roll(v, by, 1), pltpu.roll(v, 128 - by, 1)
    flat = scaled_filter(near[2], v, far[2], coarse_along_y)
    other = scaled_filter(
        jnp.where(even, near[1], near[3]),
        jnp.where(even, far[1], near[1]),
        jnp.where(even, far[3], far[1]),
        coarse_along_y,
    )
    behind = jnp.where(even, pltpu.roll(other, 1, 0), other)
    beyond = jnp.where(even, other, pltpu.roll(other, 7, 0))
    return scaled_filter(behind, flat, beyond, coarse_along_x)


def chain_kernel(received, send_out, history):
    even = even_lanes()
    depth = range(16)
    middle = 1.0
    for kind in (coarse_along_z, coarse_along_x, coarse_along_y):
        middle *= weights_of(kind)[1]
    rates = [received[16 * (z % 2) + z // 2, 16:24] for z in depth]
    drops = [1.0 - rate for rate in rates]
    rates = [middle * rate for rate in rates]

    def term(step):
        return [received[8 * step + z // 2, 8 * (z % 2) : 8 * (z % 2) + 8] for z in depth]

    def keep(step, layers):
        for z in depth:
            history[step, z] = layers[z]

    def advance(layers):
        flat = [scaled_plane_filter(v, even) for v in layers]
        out = []
        for z in depth:
            mixed = scaled_filter(flat[z - 1], flat[z], flat[(z + 1) % 16], coarse_along_z)
            out.append(drops[z] * layers[z] + rates[z] * mixed)
        return out

    history[0] = jnp.zeros((16, 8, 128), jnp.float32)
    layers = term(0)
    keep(1, layers)
    for step in range(1, GROUP):
        layers = [a + b for a, b in zip(advance(layers), term(step))]
        keep(step + 1, layers)

    def body(step, layers):
        layers = advance(layers)
        keep(step + 1, layers)
        return tuple(layers)

    mine = lax.axis_index("z")
    lax.fori_loop(GROUP, STEPS - GROUP * mine, body, tuple(layers))
    place = lax.axis_index("h") * 2 + lax.axis_index("c")
    first = (lax.axis_index("l") * 4 + lax.axis_index("y")) * 2
    for target in range(8):
        begin = jnp.where(mine <= target, GROUP * (target - mine) + place, 0)
        finish = jnp.where(mine <= target, GROUP * (target - mine) + place + 1, 0)
        if target == 0:
            begin = jnp.where(place == 0, STEPS - GROUP * mine, begin)
        send_out[target, 0:16] = history[begin, pl.ds(first, 2)].reshape(16, 128)
        send_out[target, 16:32] = history[finish, pl.ds(first, 2)].reshape(16, 128)


def add_spread(out, smooth, first, layer, even):
    low = jnp.where(even, layer, pltpu.roll(layer, 1, 1))
    high = jnp.where(even, pltpu.roll(layer, 127, 1), layer)
    for plane in (0, 32):
        for at, value in ((0, low), (1, low), (2, high), (3, high)):
            rows = pl.ds(first + plane + at, 8, stride=4)
            out[rows, :] = smooth[rows, :] + value


def finish_kernel(received, smooth, smooth_before, ends_out, starts_out):
    even = even_lanes()
    total = received[0]
    for source in range(1, 8):
        total = total + received[source]
    for i in range(2):
        add_spread(starts_out, smooth_before, 64 * i, total[8 * i : 8 * i + 8], even)
        add_spread(ends_out, smooth, 64 * i, total[16 + 8 * i : 24 + 8 * i], even)


def array(*shape):
    return jax.ShapeDtypeStruct(shape, jnp.float32)


def local(kernel, operands, outputs, scratch, operations, out_space):
    return pl.pallas_call(
        kernel,
        out_shape=outputs,
        in_specs=[pl.BlockSpec(memory_space=pltpu.VMEM)] * len(operands),
        out_specs=jax.tree.map(lambda _: pl.BlockSpec(memory_space=out_space), outputs),
        scratch_shapes=[pltpu.VMEM(shape, jnp.float32) for shape in scratch],
        cost_estimate=pl.CostEstimate(
            flops=operations, bytes_accessed=4 * sum(a.size for a in operands), transcendentals=0
        ),
        compiler_params=pltpu.CompilerParams(vmem_limit_bytes=16 * 2**20),
    )(*operands)


def per_device(starts, cell_rates):
    own = jnp.concatenate([starts.reshape(128, 128), cell_rates.reshape(128, 128)], axis=0)
    low = lax.ppermute(own, GRID, [(i, (i + 1) % 8) for i in range(8)])
    high = lax.ppermute(own, GRID, [((i + 1) % 8, i) for i in range(8)])
    smooth, message = local(
        fine_kernel,
        (own, low, high),
        (array(128, 128), array(32, 24, 128)),
        [(384, 128), (128, 128), (128, 128)],
        4_000_000,
        pltpu.VMEM,
    )
    smooth_before = lax.ppermute(smooth, SLAB, [(i, (i + 1) % 32) for i in range(32)])
    gathered = lax.all_to_all(message, PLANE, 0, 0, tiled=True)
    pieces = local(
        chain_kernel,
        (gathered,),
        array(8, 32, 128),
        [(STEPS + 1, 16, 8, 128)],
        12_000_000,
        pltpu.VMEM,
    )
    pieces, smooth_before = lax.optimization_barrier((pieces, smooth_before))
    shares = lax.all_to_all(pieces, ("z",), 0, 0, tiled=True)
    ends, nexts = local(
        finish_kernel,
        (shares, smooth, smooth_before),
        (array(128, 128), array(128, 128)),
        [],
        200_000,
        pltpu.VMEM,
    )
    return ends.reshape(1, 4, 32, 128), nexts.reshape(1, 4, 32, 128)


def solution(mesh):
    fine_mesh = Mesh(mesh.devices.reshape(8, 2, 2, 2, 4), AXES)
    state = P(SLAB, GRID, None, None)
    return jax.shard_map(
        per_device,
        mesh=fine_mesh,
        in_specs=(state, P(GRID, None, None)),
        out_specs=(state, state),
        check_vma=False,
    )
```

```python
import jax
import jax.numpy as jnp
from jax import lax
from jax.experimental import pallas as pl
from jax.experimental.pallas import tpu as pltpu
from jax.sharding import Mesh, PartitionSpec as P

FINE = 4
STEPS = 32
GROUP = 4

fine_along_z = (0.1, 0.12)
fine_along_x = (0.15, 0.12)
fine_along_y = (0.2, 0.12)
coarse_along_z = (0.2, 0.25)
coarse_along_x = (0.3, 0.25)
coarse_along_y = (0.4, 0.25)

AXES = ("z", "h", "c", "l", "y")
SLAB = ("z", "h", "c")
GRID = ("l", "y")
PLANE = ("h", "c", "l", "y")


def weights_of(kind):
    courant, diffuse = kind
    return diffuse + 0.5 * courant, 1.0 - 2.0 * diffuse, diffuse - 0.5 * courant


def line_filter(behind, middle, beyond, kind):
    a, b, c = weights_of(kind)
    return a * behind + b * middle + c * beyond


def even_lanes():
    return lax.broadcasted_iota(jnp.int32, (8, 128), 1) % 2 == 0


def packed_plane_filter(v, even):
    v = line_filter(pltpu.roll(v, 2, 1), v, pltpu.roll(v, 126, 1), coarse_along_y)
    right, left = pltpu.roll(v, 1, 1), pltpu.roll(v, 127, 1)
    behind = jnp.where(even, pltpu.roll(left, 1, 0), right)
    beyond = jnp.where(even, left, pltpu.roll(right, 7, 0))
    return line_filter(behind, v, beyond, coarse_along_x)


def packed_layer(ref, first, even):
    def rows(at):
        near = ref[pl.ds(first + at, 8, stride=4), :] + ref[pl.ds(first + at + 1, 8, stride=4), :]
        far = ref[pl.ds(first + 32 + at, 8, stride=4), :] + ref[pl.ds(first + 33 + at, 8, stride=4), :]
        return near + far

    low, high = rows(0), rows(2)
    return 0.125 * jnp.where(even, low + pltpu.roll(low, 127, 1), high + pltpu.roll(high, 1, 1))


def halo_kernel(start, rates, up, down, done):
    copies = [
        pltpu.make_async_copy(source, target, done.at[i])
        for i, (source, target) in enumerate(
            (
                (start, up.at[0:128]),
                (start, down.at[0:128]),
                (rates.at[32:128], up.at[128:224]),
                (rates.at[0:96], down.at[128:224]),
            )
        )
    ]
    for copy in copies:
        copy.start()
    for copy in copies:
        copy.wait()


def fine_kernel(up, down, low, high, smooth_out, send_out, wide, ends, rates):
    even = even_lanes()
    is_first = (lax.axis_index("z") == 0) & (lax.axis_index("h") == 0) & (lax.axis_index("c") == 0)
    wide[0:128] = low[96:224]
    wide[128:256] = down[0:128]
    wide[256:384] = high[0:128]
    rates[0:32] = down[128:160]
    rates[32:128] = up[0:96]
    current = wide[...].reshape(12, 32, 128)
    rate = jnp.concatenate([low[0:96], rates[...], high[128:224]], axis=0).reshape(10, 32, 128)
    for _ in range(FINE):
        mixed = line_filter(
            pltpu.roll(current, 1, 2), current, pltpu.roll(current, 127, 2), fine_along_y
        )
        mixed = line_filter(pltpu.roll(mixed, 1, 1), mixed, pltpu.roll(mixed, 31, 1), fine_along_x)
        mixed = line_filter(mixed[:-2], mixed[1:-1], mixed[2:], fine_along_z)
        current = current[1:-1]
        current = current + rate * (mixed - current)
        rate = rate[1:-1]
    ends[...] = current.reshape(128, 128)
    coarse = [packed_layer(wide, 64 + 64 * i, even) for i in range(4)]
    flat = [packed_plane_filter(v, even) for v in coarse]
    coarse_rates, terms = [], []
    for i in range(2):
        coarse_rates.append(packed_layer(rates, 64 * i, even))
        mixed = line_filter(flat[i], flat[i + 1], flat[i + 2], coarse_along_z)
        guess = coarse[i + 1] + coarse_rates[i] * (mixed - coarse[i + 1])
        end = packed_layer(ends, 64 * i, even)
        terms.append(end - jnp.where(is_first, jnp.zeros_like(guess), guess))
        add_spread(smooth_out, ends, 64 * i, -end, even)
    layer = jnp.where(lax.axis_index("h") == 0, coarse_rates[0], coarse_rates[1])
    layer = jnp.where(lax.axis_index("c") == 0, layer, pltpu.roll(layer, 4, 0))
    for i in range(2):
        for half in range(2):
            rows = terms[i][4 * half : 4 * half + 4]
            send_out[:, 2 * i + half] = jnp.broadcast_to(rows[None], (32, 4, 128))
    send_out[:, 4] = jnp.broadcast_to(layer[None, 0:4], (32, 4, 128))


def side_weights(kind):
    a, b, c = weights_of(kind)
    return a / b, c / b


def scaled_filter(behind, middle, beyond, kind):
    a, c = side_weights(kind)
    return middle + (a * behind + c * beyond)


def scaled_plane_filter(v, even):
    near, far = {}, {}
    for by in (1, 2, 3):
        near[by], far[by] = pltpu.roll(v, by, 1), pltpu.roll(v, 128 - by, 1)
    flat = scaled_filter(near[2], v, far[2], coarse_along_y)
    other = scaled_filter(
        jnp.where(even, near[1], near[3]),
        jnp.where(even, far[1], near[1]),
        jnp.where(even, far[3], far[1]),
        coarse_along_y,
    )
    behind = jnp.where(even, pltpu.roll(other, 1, 0), other)
    beyond = jnp.where(even, other, pltpu.roll(other, 7, 0))
    return scaled_filter(behind, flat, beyond, coarse_along_x)


def chain_kernel(received, send_out, history):
    even = even_lanes()
    depth = range(16)

    def joined(first, second):
        return jnp.concatenate([received[first], received[second]], axis=0)

    middle = 1.0
    for kind in (coarse_along_z, coarse_along_x, coarse_along_y):
        middle *= weights_of(kind)[1]
    rates = [joined((16 * (z % 2) + z // 2, 4), (16 * (z % 2) + 8 + z // 2, 4)) for z in depth]
    drops = [1.0 - rate for rate in rates]
    rates = [middle * rate for rate in rates]

    def term(step):
        at = [(8 * step + z // 2, 2 * (z % 2)) for z in depth]
        return [joined((source, part), (source, part + 1)) for source, part in at]

    def keep(step, layers):
        for z in depth:
            history[step, z] = layers[z]

    def advance(layers):
        flat = [scaled_plane_filter(v, even) for v in layers]
        out = []
        for z in depth:
            mixed = scaled_filter(flat[z - 1], flat[z], flat[(z + 1) % 16], coarse_along_z)
            out.append(drops[z] * layers[z] + rates[z] * mixed)
        return out

    history[0] = jnp.zeros((16, 8, 128), jnp.float32)
    layers = term(0)
    keep(1, layers)
    for step in range(1, GROUP):
        layers = [a + b for a, b in zip(advance(layers), term(step))]
        keep(step + 1, layers)

    def body(step, layers):
        layers = advance(layers)
        keep(step + 1, layers)
        return tuple(layers)

    mine = lax.axis_index("z")
    lax.fori_loop(GROUP, STEPS - GROUP * mine, body, tuple(layers))
    place = lax.axis_index("h") * 2 + lax.axis_index("c")
    first = (lax.axis_index("l") * 4 + lax.axis_index("y")) * 2
    for target in range(8):
        begin = jnp.where(mine <= target, GROUP * (target - mine) + place, 0)
        finish = jnp.where(mine <= target, GROUP * (target - mine) + place + 1, 0)
        if target == 0:
            begin = jnp.where(place == 0, STEPS - GROUP * mine, begin)
        send_out[target, 0:16] = history[begin, pl.ds(first, 2)].reshape(16, 128)
        send_out[target, 16:32] = history[finish, pl.ds(first, 2)].reshape(16, 128)


def add_spread(out, smooth, first, layer, even):
    low = jnp.where(even, layer, pltpu.roll(layer, 1, 1))
    high = jnp.where(even, pltpu.roll(layer, 127, 1), layer)
    for plane in (0, 32):
        for at, value in ((0, low), (1, low), (2, high), (3, high)):
            rows = pl.ds(first + plane + at, 8, stride=4)
            out[rows, :] = smooth[rows, :] + value


def finish_kernel(received, smooth, smooth_before, ends_out, starts_out):
    even = even_lanes()
    total = received[0]
    for source in range(1, 8):
        total = total + received[source]
    for i in range(2):
        add_spread(starts_out, smooth_before, 64 * i, total[8 * i : 8 * i + 8], even)
        add_spread(ends_out, smooth, 64 * i, total[16 + 8 * i : 24 + 8 * i], even)


def array(*shape):
    return jax.ShapeDtypeStruct(shape, jnp.float32)


def local(kernel, operands, outputs, scratch, operations, space=pltpu.VMEM, sent=True):
    if sent:
        outputs = jax.tree.map(lambda a: pltpu.VMEM(a.shape, a.dtype), outputs)
    return pl.pallas_call(
        kernel,
        out_shape=outputs,
        in_specs=[pl.BlockSpec(memory_space=space)] * len(operands),
        out_specs=jax.tree.map(lambda _: pl.BlockSpec(memory_space=pltpu.VMEM), outputs),
        scratch_shapes=scratch,
        cost_estimate=pl.CostEstimate(
            flops=operations, bytes_accessed=4 * sum(a.size for a in operands), transcendentals=0
        ),
        compiler_params=pltpu.CompilerParams(vmem_limit_bytes=16 * 2**20),
    )(*operands)


def scratch(*shape):
    return pltpu.VMEM(shape, jnp.float32)


def per_device(starts, cell_rates):
    start, rates = starts.reshape(128, 128), cell_rates.reshape(128, 128)
    own = jnp.concatenate([rates, start, rates], axis=0)
    up, down = own[32:256], own[128:352]
    low = lax.ppermute(up, GRID, [(i, (i + 1) % 8) for i in range(8)])
    high = lax.ppermute(down, GRID, [((i + 1) % 8, i) for i in range(8)])
    smooth, message = local(
        fine_kernel,
        (up, down, low, high),
        (array(128, 128), array(32, 5, 4, 128)),
        [scratch(384, 128), scratch(128, 128), scratch(128, 128)],
        4_000_000,
    )
    gathered = lax.all_to_all(message, PLANE, 0, 0, tiled=True)
    pieces = local(
        chain_kernel,
        (gathered,),
        array(8, 32, 128),
        [scratch(STEPS + 1, 16, 8, 128)],
        12_000_000,
    )
    pieces, smooth = lax.optimization_barrier((pieces, smooth))
    smooth_before = lax.ppermute(smooth, SLAB, [(i, (i + 1) % 32) for i in range(32)])
    shares = lax.all_to_all(pieces, ("z",), 0, 0, tiled=True)
    ends, nexts = local(
        finish_kernel,
        (shares, smooth, smooth_before),
        (array(128, 128), array(128, 128)),
        [],
        200_000,
        sent=False,
    )
    return ends.reshape(1, 4, 32, 128), nexts.reshape(1, 4, 32, 128)


def solution(mesh):
    fine_mesh = Mesh(mesh.devices.reshape(8, 2, 2, 2, 4), AXES)
    state = P(SLAB, GRID, None, None)
    return jax.shard_map(
        per_device,
        mesh=fine_mesh,
        in_specs=(state, P(GRID, None, None)),
        out_specs=(state, state),
        check_vma=False,
    )
```

```python
import jax
import jax.numpy as jnp
from jax import lax
from jax.experimental import pallas as pl
from jax.experimental.pallas import tpu as pltpu
from jax.sharding import Mesh, PartitionSpec as P

FINE = 4
STEPS = 32
GROUP = 4

fine_along_z = (0.1, 0.12)
fine_along_x = (0.15, 0.12)
fine_along_y = (0.2, 0.12)
coarse_along_z = (0.2, 0.25)
coarse_along_x = (0.3, 0.25)
coarse_along_y = (0.4, 0.25)

AXES = ("z", "h", "c", "l", "y")
SLAB = ("z", "h", "c")
GRID = ("l", "y")
CORES = ("h", "l", "y")


def weights_of(kind):
    courant, diffuse = kind
    return diffuse + 0.5 * courant, 1.0 - 2.0 * diffuse, diffuse - 0.5 * courant


def line_filter(behind, middle, beyond, kind):
    a, b, c = weights_of(kind)
    return a * behind + b * middle + c * beyond


def even_lanes():
    return lax.broadcasted_iota(jnp.int32, (8, 128), 1) % 2 == 0


def packed_plane_filter(v, even):
    v = line_filter(pltpu.roll(v, 2, 1), v, pltpu.roll(v, 126, 1), coarse_along_y)
    right, left = pltpu.roll(v, 1, 1), pltpu.roll(v, 127, 1)
    behind = jnp.where(even, pltpu.roll(left, 1, 0), right)
    beyond = jnp.where(even, left, pltpu.roll(right, 7, 0))
    return line_filter(behind, v, beyond, coarse_along_x)


def packed_layer(ref, first, even):
    def rows(at):
        near = ref[pl.ds(first + at, 8, stride=4), :] + ref[pl.ds(first + at + 1, 8, stride=4), :]
        far = ref[pl.ds(first + 32 + at, 8, stride=4), :] + ref[pl.ds(first + 33 + at, 8, stride=4), :]
        return near + far

    low, high = rows(0), rows(2)
    return 0.125 * jnp.where(even, low + pltpu.roll(low, 127, 1), high + pltpu.roll(high, 1, 1))


def fine_kernel(one, two, from_one, from_two, smooth_out, send_out, wide, ends, all_rates, rates):
    even = even_lanes()
    is_first = (lax.axis_index("z") == 0) & (lax.axis_index("h") == 0) & (lax.axis_index("c") == 0)
    is_even = lax.axis_index("y") % 2 == 0
    wide[pl.ds(pl.multiple_of(jnp.where(is_even, 256, 0), 32), 128)] = from_one[96:224]
    wide[128:256] = one[96:224]
    wide[pl.ds(pl.multiple_of(jnp.where(is_even, 0, 256), 32), 128)] = from_two[0:128]
    rates[0:32] = jnp.where(is_even, two[128:160], one[0:32])
    rates[32:128] = jnp.where(is_even, one[0:96], two[128:224])
    all_rates[pl.ds(pl.multiple_of(jnp.where(is_even, 224, 0), 32), 96)] = from_one[0:96]
    all_rates[96:224] = rates[...]
    all_rates[pl.ds(pl.multiple_of(jnp.where(is_even, 0, 224), 32), 96)] = from_two[128:224]
    current = wide[...].reshape(12, 32, 128)
    rate = all_rates[...].reshape(10, 32, 128)
    for _ in range(FINE):
        mixed = line_filter(
            pltpu.roll(current, 1, 2), current, pltpu.roll(current, 127, 2), fine_along_y
        )
        mixed = line_filter(pltpu.roll(mixed, 1, 1), mixed, pltpu.roll(mixed, 31, 1), fine_along_x)
        mixed = line_filter(mixed[:-2], mixed[1:-1], mixed[2:], fine_along_z)
        current = current[1:-1]
        current = current + rate * (mixed - current)
        rate = rate[1:-1]
    ends[...] = current.reshape(128, 128)
    coarse = [packed_layer(wide, 64 + 64 * i, even) for i in range(4)]
    flat = [packed_plane_filter(v, even) for v in coarse]
    coarse_rates, terms = [], []
    for i in range(2):
        coarse_rates.append(packed_layer(rates, 64 * i, even))
        mixed = line_filter(flat[i], flat[i + 1], flat[i + 2], coarse_along_z)
        guess = coarse[i + 1] + coarse_rates[i] * (mixed - coarse[i + 1])
        end = packed_layer(ends, 64 * i, even)
        terms.append(end - jnp.where(is_first, jnp.zeros_like(guess), guess))
        add_spread(smooth_out, ends, 64 * i, -end, even)
    layer = jnp.where(lax.axis_index("h") == 0, coarse_rates[0], coarse_rates[1])
    layer = jnp.where(lax.axis_index("c") == 0, layer, pltpu.roll(layer, 4, 0))
    for i in range(2):
        for half in range(2):
            rows = terms[i][4 * half : 4 * half + 4]
            send_out[:, 2 * i + half] = jnp.broadcast_to(rows[None], (16, 4, 128))
    send_out[:, 4] = jnp.broadcast_to(layer[None, 0:4], (16, 4, 128))


def side_weights(kind):
    a, b, c = weights_of(kind)
    return a / b, c / b


def scaled_filter(behind, middle, beyond, kind):
    a, c = side_weights(kind)
    return middle + (a * behind + c * beyond)


def scaled_plane_filter(v, even):
    near, far = {}, {}
    for by in (1, 2, 3):
        near[by], far[by] = pltpu.roll(v, by, 1), pltpu.roll(v, 128 - by, 1)
    flat = scaled_filter(near[2], v, far[2], coarse_along_y)
    other = scaled_filter(
        jnp.where(even, near[1], near[3]),
        jnp.where(even, far[1], near[1]),
        jnp.where(even, far[3], far[1]),
        coarse_along_y,
    )
    behind = jnp.where(even, pltpu.roll(other, 1, 0), other)
    beyond = jnp.where(even, other, pltpu.roll(other, 7, 0))
    return scaled_filter(behind, flat, beyond, coarse_along_x)


def chain_kernel(received, from_core, send_out, history):
    even = even_lanes()
    is_first_core = lax.axis_index("c") == 0
    depth = range(16)

    def piece(source, part):
        far, core, place = source
        first, second = (received, from_core) if core == 0 else (from_core, received)
        at = (8 * far + place, part)
        return jnp.where(is_first_core, first[at], second[at])

    def joined(first, second, part, next_part):
        return jnp.concatenate([piece(first, part), piece(second, next_part)], axis=0)

    middle = 1.0
    for kind in (coarse_along_z, coarse_along_x, coarse_along_y):
        middle *= weights_of(kind)[1]
    rates = [joined((z % 2, 0, z // 2), (z % 2, 1, z // 2), 4, 4) for z in depth]
    drops = [1.0 - rate for rate in rates]
    rates = [middle * rate for rate in rates]

    def term(step):
        at = [((step // 2, step % 2, z // 2), 2 * (z % 2)) for z in depth]
        return [joined(source, source, part, part + 1) for source, part in at]

    def keep(step, layers):
        for z in depth:
            history[step, z] = layers[z]

    def advance(layers):
        flat = [scaled_plane_filter(v, even) for v in layers]
        out = []
        for z in depth:
            mixed = scaled_filter(flat[z - 1], flat[z], flat[(z + 1) % 16], coarse_along_z)
            out.append(drops[z] * layers[z] + rates[z] * mixed)
        return out

    history[0] = jnp.zeros((16, 8, 128), jnp.float32)
    layers = term(0)
    keep(1, layers)
    for step in range(1, GROUP):
        layers = [a + b for a, b in zip(advance(layers), term(step))]
        keep(step + 1, layers)

    def body(step, layers):
        layers = advance(layers)
        keep(step + 1, layers)
        return tuple(layers)

    mine = lax.axis_index("z")
    lax.fori_loop(GROUP, STEPS - GROUP * mine, body, tuple(layers))
    place = lax.axis_index("h") * 2 + lax.axis_index("c")
    first = (lax.axis_index("l") * 4 + lax.axis_index("y")) * 2
    for target in range(8):
        begin = jnp.where(mine <= target, GROUP * (target - mine) + place, 0)
        finish = jnp.where(mine <= target, GROUP * (target - mine) + place + 1, 0)
        if target == 0:
            begin = jnp.where(place == 0, STEPS - GROUP * mine, begin)
        send_out[target, 0:16] = history[begin, pl.ds(first, 2)].reshape(16, 128)
        send_out[target, 16:32] = history[finish, pl.ds(first, 2)].reshape(16, 128)


def add_spread(out, smooth, first, layer, even):
    low = jnp.where(even, layer, pltpu.roll(layer, 1, 1))
    high = jnp.where(even, pltpu.roll(layer, 127, 1), layer)
    for plane in (0, 32):
        for at, value in ((0, low), (1, low), (2, high), (3, high)):
            rows = pl.ds(first + plane + at, 8, stride=4)
            out[rows, :] = smooth[rows, :] + value


def finish_kernel(received, smooth, smooth_before, ends_out, starts_out):
    even = even_lanes()
    total = received[0]
    for source in range(1, 8):
        total = total + received[source]
    for i in range(2):
        add_spread(starts_out, smooth_before, 64 * i, total[8 * i : 8 * i + 8], even)
        add_spread(ends_out, smooth, 64 * i, total[16 + 8 * i : 24 + 8 * i], even)


def array(*shape):
    return jax.ShapeDtypeStruct(shape, jnp.float32)


def local(kernel, operands, outputs, buffers, operations, sent=True):
    if sent:
        outputs = jax.tree.map(lambda a: pltpu.VMEM(a.shape, a.dtype), outputs)
    return pl.pallas_call(
        kernel,
        out_shape=outputs,
        in_specs=[pl.BlockSpec(memory_space=pltpu.VMEM)] * len(operands),
        out_specs=jax.tree.map(lambda _: pl.BlockSpec(memory_space=pltpu.VMEM), outputs),
        scratch_shapes=buffers,
        cost_estimate=pl.CostEstimate(
            flops=operations, bytes_accessed=4 * sum(a.size for a in operands), transcendentals=0
        ),
        compiler_params=pltpu.CompilerParams(vmem_limit_bytes=16 * 2**20),
    )(*operands)


def scratch(*shape):
    return pltpu.VMEM(shape, jnp.float32)


def per_device(starts, cell_rates):
    start, rates = starts.reshape(128, 128), cell_rates.reshape(128, 128)
    is_even = lax.axis_index("y") % 2 == 0
    for_below, for_above = rates[:96], rates[32:]
    own = jnp.concatenate(
        [
            jnp.where(is_even, for_above, for_below),
            start,
            jnp.where(is_even, for_below, for_above),
        ],
        axis=0,
    )
    one, two = own[:224], own[96:]
    pairs = [(i, i ^ 1) for i in range(8)]
    others = [(i, (i - 1 + 2 * (i % 2)) % 8) for i in range(8)]
    from_one = lax.ppermute(one, GRID, pairs)
    from_two = lax.ppermute(two, GRID, others)
    smooth, message = local(
        fine_kernel,
        (one, two, from_one, from_two),
        (array(128, 128), array(16, 5, 4, 128)),
        [scratch(384, 128), scratch(128, 128), scratch(320, 128), scratch(128, 128)],
        4_000_000,
    )
    gathered = lax.all_to_all(message, CORES, 0, 0, tiled=True)
    from_core = lax.ppermute(gathered, ("c",), [(0, 1), (1, 0)])
    pieces = local(
        chain_kernel,
        (gathered, from_core),
        array(8, 32, 128),
        [scratch(STEPS + 1, 16, 8, 128)],
        12_000_000,
    )
    pieces, smooth = lax.optimization_barrier((pieces, smooth))
    smooth_before = lax.ppermute(smooth, SLAB, [(i, (i + 1) % 32) for i in range(32)])
    shares = lax.all_to_all(pieces, ("z",), 0, 0, tiled=True)
    ends, nexts = local(
        finish_kernel,
        (shares, smooth, smooth_before),
        (array(128, 128), array(128, 128)),
        [],
        200_000,
        sent=False,
    )
    return ends.reshape(1, 4, 32, 128), nexts.reshape(1, 4, 32, 128)


def solution(mesh):
    fine_mesh = Mesh(mesh.devices.reshape(8, 2, 2, 2, 4), AXES)
    state = P(SLAB, GRID, None, None)
    return jax.shard_map(
        per_device,
        mesh=fine_mesh,
        in_specs=(state, P(GRID, None, None)),
        out_specs=(state, state),
        check_vma=False,
    )
```

```python
import jax
import jax.numpy as jnp
from jax import lax
from jax.experimental import pallas as pl
from jax.experimental.pallas import tpu as pltpu
from jax.sharding import Mesh, PartitionSpec as P

FINE = 4
STEPS = 32
GROUP = 4

fine_along_z = (0.1, 0.12)
fine_along_x = (0.15, 0.12)
fine_along_y = (0.2, 0.12)
coarse_along_z = (0.2, 0.25)
coarse_along_x = (0.3, 0.25)
coarse_along_y = (0.4, 0.25)

AXES = ("z", "h", "c", "l", "y")
SLAB = ("z", "h", "c")
GRID = ("l", "y")
CORES = ("h", "l", "y")


def weights_of(kind):
    courant, diffuse = kind
    return diffuse + 0.5 * courant, 1.0 - 2.0 * diffuse, diffuse - 0.5 * courant


def line_filter(behind, middle, beyond, kind):
    a, b, c = weights_of(kind)
    return a * behind + b * middle + c * beyond


def side_weights(kind):
    a, b, c = weights_of(kind)
    return a / b, c / b


def scaled_filter(behind, middle, beyond, kind):
    a, c = side_weights(kind)
    return middle + (a * behind + c * beyond)


def even_lanes():
    return lax.broadcasted_iota(jnp.int32, (8, 128), 1) % 2 == 0


def packed_plane_filter(v, even):
    v = line_filter(pltpu.roll(v, 2, 1), v, pltpu.roll(v, 126, 1), coarse_along_y)
    right, left = pltpu.roll(v, 1, 1), pltpu.roll(v, 127, 1)
    behind = jnp.where(even, pltpu.roll(left, 1, 0), right)
    beyond = jnp.where(even, left, pltpu.roll(right, 7, 0))
    return line_filter(behind, v, beyond, coarse_along_x)


def packed_layer(ref, first, even):
    def rows(at):
        near = ref[pl.ds(first + at, 8, stride=4), :] + ref[pl.ds(first + at + 1, 8, stride=4), :]
        far = ref[pl.ds(first + 32 + at, 8, stride=4), :] + ref[pl.ds(first + 33 + at, 8, stride=4), :]
        return near + far

    low, high = rows(0), rows(2)
    return 0.125 * jnp.where(even, low + pltpu.roll(low, 127, 1), high + pltpu.roll(high, 1, 1))


def fine_kernel(one, two, from_one, from_two, smooth_out, send_out, wide, ends, all_rates, rates):
    even = even_lanes()
    is_first = (lax.axis_index("z") == 0) & (lax.axis_index("h") == 0) & (lax.axis_index("c") == 0)
    is_even = lax.axis_index("y") % 2 == 0
    wide[pl.ds(pl.multiple_of(jnp.where(is_even, 256, 0), 32), 128)] = from_one[96:224]
    wide[128:256] = one[96:224]
    wide[pl.ds(pl.multiple_of(jnp.where(is_even, 0, 256), 32), 128)] = from_two[0:128]
    rates[0:32] = jnp.where(is_even, two[128:160], one[0:32])
    rates[32:128] = jnp.where(is_even, one[0:96], two[128:224])
    all_rates[pl.ds(pl.multiple_of(jnp.where(is_even, 224, 0), 32), 96)] = from_one[0:96]
    all_rates[96:224] = rates[...]
    all_rates[pl.ds(pl.multiple_of(jnp.where(is_even, 0, 224), 32), 96)] = from_two[128:224]
    current = wide[...].reshape(12, 32, 128)
    rate = all_rates[...].reshape(10, 32, 128)
    middle = 1.0
    for kind in (fine_along_z, fine_along_x, fine_along_y):
        middle *= weights_of(kind)[1]
    drop, gain = 1.0 - rate, middle * rate
    for _ in range(FINE):
        mixed = scaled_filter(current[:-2], current[1:-1], current[2:], fine_along_z)
        mixed = scaled_filter(
            pltpu.roll(mixed, 1, 1), mixed, pltpu.roll(mixed, 31, 1), fine_along_x
        )
        mixed = scaled_filter(
            pltpu.roll(mixed, 1, 2), mixed, pltpu.roll(mixed, 127, 2), fine_along_y
        )
        current = drop * current[1:-1] + gain * mixed
        drop, gain = drop[1:-1], gain[1:-1]
    ends[...] = current.reshape(128, 128)
    coarse = [packed_layer(wide, 64 + 64 * i, even) for i in range(4)]
    flat = [packed_plane_filter(v, even) for v in coarse]
    coarse_rates, terms = [], []
    for i in range(2):
        coarse_rates.append(packed_layer(rates, 64 * i, even))
        mixed = line_filter(flat[i], flat[i + 1], flat[i + 2], coarse_along_z)
        guess = coarse[i + 1] + coarse_rates[i] * (mixed - coarse[i + 1])
        end = packed_layer(ends, 64 * i, even)
        terms.append(end - jnp.where(is_first, jnp.zeros_like(guess), guess))
        add_spread(smooth_out, ends, 64 * i, -end, even)
    layer = jnp.where(lax.axis_index("h") == 0, coarse_rates[0], coarse_rates[1])
    layer = jnp.where(lax.axis_index("c") == 0, layer, pltpu.roll(layer, 4, 0))
    for i in range(2):
        for half in range(2):
            rows = terms[i][4 * half : 4 * half + 4]
            send_out[:, 2 * i + half] = jnp.broadcast_to(rows[None], (16, 4, 128))
    send_out[:, 4] = jnp.broadcast_to(layer[None, 0:4], (16, 4, 128))


def spread_pair(v, even):
    return jnp.where(even, v, pltpu.roll(v, 1, 1)), jnp.where(even, pltpu.roll(v, 127, 1), v)


def pair_filter(pair):
    low, high = (
        scaled_filter(pltpu.roll(v, 2, 1), v, pltpu.roll(v, 126, 1), coarse_along_y) for v in pair
    )
    return (
        scaled_filter(pltpu.roll(high, 1, 0), low, high, coarse_along_x),
        scaled_filter(low, high, pltpu.roll(low, 7, 0), coarse_along_x),
    )


def chain_kernel(received, from_core, send_out, history):
    even = even_lanes()
    is_first_core = lax.axis_index("c") == 0
    depth = range(16)

    def piece(source, part):
        far, core, place = source
        first, second = (received, from_core) if core == 0 else (from_core, received)
        at = (8 * far + place, part)
        return jnp.where(is_first_core, first[at], second[at])

    def joined(first, second, part, next_part):
        return jnp.concatenate([piece(first, part), piece(second, next_part)], axis=0)

    middle = 1.0
    for kind in (coarse_along_z, coarse_along_x, coarse_along_y):
        middle *= weights_of(kind)[1]
    rates = [joined((z % 2, 0, z // 2), (z % 2, 1, z // 2), 4, 4) for z in depth]
    rates = [spread_pair(rate, even) for rate in rates]
    drops = [[1.0 - rate for rate in pair] for pair in rates]
    rates = [[middle * rate for rate in pair] for pair in rates]

    def term(step):
        at = [((step // 2, step % 2, z // 2), 2 * (z % 2)) for z in depth]
        return [joined(source, source, part, part + 1) for source, part in at]

    def keep(step, layers):
        for z in depth:
            history[step, z] = jnp.where(even, *layers[z])

    def advance(layers):
        flat = [pair_filter(pair) for pair in layers]
        out = []
        for z in depth:
            behind, here, beyond = flat[z - 1], flat[z], flat[(z + 1) % 16]
            mixed = [scaled_filter(*trio, coarse_along_z) for trio in zip(behind, here, beyond)]
            out.append([drops[z][i] * layers[z][i] + rates[z][i] * mixed[i] for i in range(2)])
        return out

    history[0] = jnp.zeros((16, 8, 128), jnp.float32)
    layers = [spread_pair(v, even) for v in term(0)]
    keep(1, layers)
    for step in range(1, GROUP):
        added = [spread_pair(v, even) for v in term(step)]
        layers = [[a + b for a, b in zip(*both)] for both in zip(advance(layers), added)]
        keep(step + 1, layers)

    def body(step, layers):
        layers = advance(layers)
        keep(step + 1, layers)
        return layers

    mine = lax.axis_index("z")
    lax.fori_loop(GROUP, STEPS - GROUP * mine, body, layers)
    place = lax.axis_index("h") * 2 + lax.axis_index("c")
    first = (lax.axis_index("l") * 4 + lax.axis_index("y")) * 2
    for target in range(8):
        begin = jnp.where(mine <= target, GROUP * (target - mine) + place, 0)
        finish = jnp.where(mine <= target, GROUP * (target - mine) + place + 1, 0)
        if target == 0:
            begin = jnp.where(place == 0, STEPS - GROUP * mine, begin)
        send_out[target, 0:16] = history[begin, pl.ds(first, 2)].reshape(16, 128)
        send_out[target, 16:32] = history[finish, pl.ds(first, 2)].reshape(16, 128)


def add_spread(out, smooth, first, layer, even):
    low = jnp.where(even, layer, pltpu.roll(layer, 1, 1))
    high = jnp.where(even, pltpu.roll(layer, 127, 1), layer)
    for plane in (0, 32):
        for at, value in ((0, low), (1, low), (2, high), (3, high)):
            rows = pl.ds(first + plane + at, 8, stride=4)
            out[rows, :] = smooth[rows, :] + value


def finish_kernel(received, smooth, smooth_before, ends_out, starts_out):
    even = even_lanes()
    total = received[0]
    for source in range(1, 8):
        total = total + received[source]
    for i in range(2):
        add_spread(starts_out, smooth_before, 64 * i, total[8 * i : 8 * i + 8], even)
        add_spread(ends_out, smooth, 64 * i, total[16 + 8 * i : 24 + 8 * i], even)


def array(*shape):
    return jax.ShapeDtypeStruct(shape, jnp.float32)


def local(kernel, operands, outputs, buffers, operations, sent=True):
    if sent:
        outputs = jax.tree.map(lambda a: pltpu.VMEM(a.shape, a.dtype), outputs)
    return pl.pallas_call(
        kernel,
        out_shape=outputs,
        in_specs=[pl.BlockSpec(memory_space=pltpu.VMEM)] * len(operands),
        out_specs=jax.tree.map(lambda _: pl.BlockSpec(memory_space=pltpu.VMEM), outputs),
        scratch_shapes=buffers,
        cost_estimate=pl.CostEstimate(
            flops=operations, bytes_accessed=4 * sum(a.size for a in operands), transcendentals=0
        ),
        compiler_params=pltpu.CompilerParams(vmem_limit_bytes=16 * 2**20),
    )(*operands)


def scratch(*shape):
    return pltpu.VMEM(shape, jnp.float32)


def per_device(starts, cell_rates):
    start, rates = starts.reshape(128, 128), cell_rates.reshape(128, 128)
    is_even = lax.axis_index("y") % 2 == 0
    for_below, for_above = rates[:96], rates[32:]
    own = jnp.concatenate(
        [
            jnp.where(is_even, for_above, for_below),
            start,
            jnp.where(is_even, for_below, for_above),
        ],
        axis=0,
    )
    one, two = own[:224], own[96:]
    pairs = [(i, i ^ 1) for i in range(8)]
    others = [(i, (i - 1 + 2 * (i % 2)) % 8) for i in range(8)]
    from_one = lax.ppermute(one, GRID, pairs)
    from_two = lax.ppermute(two, GRID, others)
    smooth, message = local(
        fine_kernel,
        (one, two, from_one, from_two),
        (array(128, 128), array(16, 5, 4, 128)),
        [scratch(384, 128), scratch(128, 128), scratch(320, 128), scratch(128, 128)],
        4_000_000,
    )
    gathered = lax.all_to_all(message, CORES, 0, 0, tiled=True)
    from_core = lax.ppermute(gathered, ("c",), [(0, 1), (1, 0)])
    pieces = local(
        chain_kernel,
        (gathered, from_core),
        array(8, 32, 128),
        [scratch(STEPS + 1, 16, 8, 128)],
        12_000_000,
    )
    pieces, smooth = lax.optimization_barrier((pieces, smooth))
    smooth_before = lax.ppermute(smooth, SLAB, [(i, (i + 1) % 32) for i in range(32)])
    shares = lax.all_to_all(pieces, ("z",), 0, 0, tiled=True)
    ends, nexts = local(
        finish_kernel,
        (shares, smooth, smooth_before),
        (array(128, 128), array(128, 128)),
        [],
        200_000,
        sent=False,
    )
    return ends.reshape(1, 4, 32, 128), nexts.reshape(1, 4, 32, 128)


def solution(mesh):
    fine_mesh = Mesh(mesh.devices.reshape(8, 2, 2, 2, 4), AXES)
    state = P(SLAB, GRID, None, None)
    return jax.shard_map(
        per_device,
        mesh=fine_mesh,
        in_specs=(state, P(GRID, None, None)),
        out_specs=(state, state),
        check_vma=False,
    )
```

```python
import jax
import jax.numpy as jnp
from jax import lax
from jax.experimental import pallas as pl
from jax.experimental.pallas import tpu as pltpu
from jax.sharding import Mesh, PartitionSpec as P

FINE = 4
STEPS = 32
GROUP = 4

fine_along_z = (0.1, 0.12)
fine_along_x = (0.15, 0.12)
fine_along_y = (0.2, 0.12)
coarse_along_z = (0.2, 0.25)
coarse_along_x = (0.3, 0.25)
coarse_along_y = (0.4, 0.25)

AXES = ("z", "h", "c", "l", "y")
SLAB = ("z", "h", "c")
GRID = ("l", "y")
CORES = ("h", "l", "y")


def weights_of(kind):
    courant, diffuse = kind
    return diffuse + 0.5 * courant, 1.0 - 2.0 * diffuse, diffuse - 0.5 * courant


def line_filter(behind, middle, beyond, kind):
    a, b, c = weights_of(kind)
    return a * behind + b * middle + c * beyond


def side_weights(kind):
    a, b, c = weights_of(kind)
    return a / b, c / b


def scaled_filter(behind, middle, beyond, kind):
    a, c = side_weights(kind)
    return middle + (a * behind + c * beyond)


def even_lanes():
    return lax.broadcasted_iota(jnp.int32, (8, 128), 1) % 2 == 0


def packed_plane_filter(v, even):
    v = line_filter(pltpu.roll(v, 2, 1), v, pltpu.roll(v, 126, 1), coarse_along_y)
    right, left = pltpu.roll(v, 1, 1), pltpu.roll(v, 127, 1)
    behind = jnp.where(even, pltpu.roll(left, 1, 0), right)
    beyond = jnp.where(even, left, pltpu.roll(right, 7, 0))
    return line_filter(behind, v, beyond, coarse_along_x)


def packed_layer(ref, first, even):
    def rows(at):
        near = ref[pl.ds(first + at, 8, stride=4), :] + ref[pl.ds(first + at + 1, 8, stride=4), :]
        far = ref[pl.ds(first + 32 + at, 8, stride=4), :] + ref[pl.ds(first + 33 + at, 8, stride=4), :]
        return near + far

    low, high = rows(0), rows(2)
    return 0.125 * jnp.where(even, low + pltpu.roll(low, 127, 1), high + pltpu.roll(high, 1, 1))


def fine_kernel(one, two, from_one, from_two, smooth_out, send_out, wide, ends, all_rates, rates):
    even = even_lanes()
    is_first = (lax.axis_index("z") == 0) & (lax.axis_index("h") == 0) & (lax.axis_index("c") == 0)
    is_even = lax.axis_index("y") % 2 == 0
    wide[pl.ds(pl.multiple_of(jnp.where(is_even, 256, 0), 32), 128)] = from_one[96:224]
    wide[128:256] = one[96:224]
    wide[pl.ds(pl.multiple_of(jnp.where(is_even, 0, 256), 32), 128)] = from_two[0:128]
    rates[0:32] = jnp.where(is_even, two[128:160], one[0:32])
    rates[32:128] = jnp.where(is_even, one[0:96], two[128:224])
    all_rates[pl.ds(pl.multiple_of(jnp.where(is_even, 224, 0), 32), 96)] = from_one[0:96]
    all_rates[96:224] = rates[...]
    all_rates[pl.ds(pl.multiple_of(jnp.where(is_even, 0, 224), 32), 96)] = from_two[128:224]
    current = wide[...].reshape(12, 32, 128)
    rate = all_rates[...].reshape(10, 32, 128)
    middle = 1.0
    for kind in (fine_along_z, fine_along_x, fine_along_y):
        middle *= weights_of(kind)[1]
    drop, gain = 1.0 - rate, middle * rate
    for _ in range(FINE):
        mixed = scaled_filter(current[:-2], current[1:-1], current[2:], fine_along_z)
        mixed = scaled_filter(
            pltpu.roll(mixed, 1, 1), mixed, pltpu.roll(mixed, 31, 1), fine_along_x
        )
        mixed = scaled_filter(
            pltpu.roll(mixed, 1, 2), mixed, pltpu.roll(mixed, 127, 2), fine_along_y
        )
        current = drop * current[1:-1] + gain * mixed
        drop, gain = drop[1:-1], gain[1:-1]
    ends[...] = current.reshape(128, 128)
    coarse = [packed_layer(wide, 64 + 64 * i, even) for i in range(4)]
    flat = [packed_plane_filter(v, even) for v in coarse]
    coarse_rates, terms = [], []
    for i in range(2):
        coarse_rates.append(packed_layer(rates, 64 * i, even))
        mixed = line_filter(flat[i], flat[i + 1], flat[i + 2], coarse_along_z)
        guess = coarse[i + 1] + coarse_rates[i] * (mixed - coarse[i + 1])
        end = packed_layer(ends, 64 * i, even)
        terms.append(end - jnp.where(is_first, jnp.zeros_like(guess), guess))
        add_spread(smooth_out, ends, 64 * i, -end, even)
    layer = jnp.where(lax.axis_index("h") == 0, coarse_rates[0], coarse_rates[1])
    layer = jnp.where(lax.axis_index("c") == 0, layer, pltpu.roll(layer, 4, 0))
    for i in range(2):
        for half in range(2):
            rows = terms[i][4 * half : 4 * half + 4]
            send_out[:, 2 * i + half] = jnp.broadcast_to(rows[None], (16, 4, 128))
    send_out[:, 4] = jnp.broadcast_to(layer[None, 0:4], (16, 4, 128))


def spread_pair(v, even):
    return jnp.where(even, v, pltpu.roll(v, 1, 1)), jnp.where(even, pltpu.roll(v, 127, 1), v)


def pair_filter(pair):
    low, high = (
        scaled_filter(pltpu.roll(v, 2, 1), v, pltpu.roll(v, 126, 1), coarse_along_y) for v in pair
    )
    return (
        scaled_filter(pltpu.roll(high, 1, 0), low, high, coarse_along_x),
        scaled_filter(low, high, pltpu.roll(low, 7, 0), coarse_along_x),
    )


def chain_kernel(received, from_core, send_out, history):
    even = even_lanes()
    is_first_core = lax.axis_index("c") == 0
    depth = range(16)
    part = lax.axis_index("l") * 4 + lax.axis_index("y")
    places = [lax.rem(part + i, 8) for i in range(8)]

    def piece(far, core, layer, row):
        first, second = (received, from_core) if core == 0 else (from_core, received)
        at = (8 * far + places[layer // 2], row)
        return jnp.where(is_first_core, first[at], second[at])

    middle = 1.0
    for kind in (coarse_along_z, coarse_along_x, coarse_along_y):
        middle *= weights_of(kind)[1]
    rates = [jnp.concatenate([piece(z % 2, core, z, 4) for core in range(2)], axis=0) for z in depth]
    rates = [spread_pair(rate, even) for rate in rates]
    drops = [[1.0 - rate for rate in pair] for pair in rates]
    rates = [[middle * rate for rate in pair] for pair in rates]

    def term(step):
        far, core = step // 2, step % 2
        rows = [[piece(far, core, z, 2 * (z % 2) + half) for half in range(2)] for z in depth]
        return [spread_pair(jnp.concatenate(halves, axis=0), even) for halves in rows]

    def keep(step, layers):
        for z in range(2):
            history[step, z] = jnp.where(even, *layers[z])

    def advance(layers, wanted):
        needed = range(wanted[0] - 1, wanted[-1] + 2) if len(wanted) < 16 else wanted
        flat = {z % 16: pair_filter(layers[z % 16]) for z in needed}
        out = [None] * 16
        for z in (z % 16 for z in wanted):
            behind, here, beyond = flat[(z - 1) % 16], flat[z], flat[(z + 1) % 16]
            mixed = [scaled_filter(*trio, coarse_along_z) for trio in zip(behind, here, beyond)]
            out[z] = [drops[z][i] * layers[z][i] + rates[z][i] * mixed[i] for i in range(2)]
        return out

    history[0] = jnp.zeros((2, 8, 128), jnp.float32)
    layers = term(0)
    keep(1, layers)
    for step in range(1, GROUP):
        later = advance(layers, depth)
        layers = [[a + b for a, b in zip(*both)] for both in zip(later, term(step))]
        keep(step + 1, layers)

    def body(step, layers):
        layers = advance(layers, depth)
        keep(step + 1, layers)
        return layers

    mine = lax.axis_index("z")
    stop = jnp.maximum(STEPS - GROUP * mine - GROUP, GROUP)
    layers = lax.fori_loop(GROUP, stop, body, layers)
    for i in range(GROUP):
        layers = advance(layers, range(i - GROUP + 1, GROUP + 1 - i))
        keep(stop + i + 1, layers)
    place = lax.axis_index("h") * 2 + lax.axis_index("c")
    for target in range(8):
        begin = jnp.where(mine <= target, GROUP * (target - mine) + place, 0)
        finish = jnp.where(mine <= target, GROUP * (target - mine) + place + 1, 0)
        if target == 0:
            begin = jnp.where(place == 0, STEPS - GROUP * mine, begin)
        send_out[target, 0:16] = history[begin].reshape(16, 128)
        send_out[target, 16:32] = history[finish].reshape(16, 128)


def add_spread(out, smooth, first, layer, even):
    low = jnp.where(even, layer, pltpu.roll(layer, 1, 1))
    high = jnp.where(even, pltpu.roll(layer, 127, 1), layer)
    for plane in (0, 32):
        for at, value in ((0, low), (1, low), (2, high), (3, high)):
            rows = pl.ds(first + plane + at, 8, stride=4)
            out[rows, :] = smooth[rows, :] + value


def finish_kernel(received, smooth, smooth_before, ends_out, starts_out):
    even = even_lanes()
    total = received[0]
    for source in range(1, 8):
        total = total + received[source]
    for i in range(2):
        add_spread(starts_out, smooth_before, 64 * i, total[8 * i : 8 * i + 8], even)
        add_spread(ends_out, smooth, 64 * i, total[16 + 8 * i : 24 + 8 * i], even)


def array(*shape):
    return jax.ShapeDtypeStruct(shape, jnp.float32)


def local(kernel, operands, outputs, buffers, operations, sent=True):
    if sent:
        outputs = jax.tree.map(lambda a: pltpu.VMEM(a.shape, a.dtype), outputs)
    return pl.pallas_call(
        kernel,
        out_shape=outputs,
        in_specs=[pl.BlockSpec(memory_space=pltpu.VMEM)] * len(operands),
        out_specs=jax.tree.map(lambda _: pl.BlockSpec(memory_space=pltpu.VMEM), outputs),
        scratch_shapes=buffers,
        cost_estimate=pl.CostEstimate(
            flops=operations, bytes_accessed=4 * sum(a.size for a in operands), transcendentals=0
        ),
        compiler_params=pltpu.CompilerParams(vmem_limit_bytes=16 * 2**20),
    )(*operands)


def scratch(*shape):
    return pltpu.VMEM(shape, jnp.float32)


def per_device(starts, cell_rates):
    start, rates = starts.reshape(128, 128), cell_rates.reshape(128, 128)
    is_even = lax.axis_index("y") % 2 == 0
    for_below, for_above = rates[:96], rates[32:]
    own = jnp.concatenate(
        [
            jnp.where(is_even, for_above, for_below),
            start,
            jnp.where(is_even, for_below, for_above),
        ],
        axis=0,
    )
    one, two = own[:224], own[96:]
    pairs = [(i, i ^ 1) for i in range(8)]
    others = [(i, (i - 1 + 2 * (i % 2)) % 8) for i in range(8)]
    from_one = lax.ppermute(one, GRID, pairs)
    from_two = lax.ppermute(two, GRID, others)
    smooth, message = local(
        fine_kernel,
        (one, two, from_one, from_two),
        (array(128, 128), array(16, 5, 4, 128)),
        [scratch(384, 128), scratch(128, 128), scratch(320, 128), scratch(128, 128)],
        4_000_000,
    )
    gathered = lax.all_to_all(message, CORES, 0, 0, tiled=True)
    from_core = lax.ppermute(gathered, ("c",), [(0, 1), (1, 0)])
    pieces = local(
        chain_kernel,
        (gathered, from_core),
        array(8, 32, 128),
        [scratch(STEPS + 1, 2, 8, 128)],
        12_000_000,
    )
    pieces, smooth = lax.optimization_barrier((pieces, smooth))
    smooth_before = lax.ppermute(smooth, SLAB, [(i, (i + 1) % 32) for i in range(32)])
    shares = lax.all_to_all(pieces, ("z",), 0, 0, tiled=True)
    ends, nexts = local(
        finish_kernel,
        (shares, smooth, smooth_before),
        (array(128, 128), array(128, 128)),
        [],
        200_000,
        sent=False,
    )
    return ends.reshape(1, 4, 32, 128), nexts.reshape(1, 4, 32, 128)


def solution(mesh):
    fine_mesh = Mesh(mesh.devices.reshape(8, 2, 2, 2, 4), AXES)
    state = P(SLAB, GRID, None, None)
    return jax.shard_map(
        per_device,
        mesh=fine_mesh,
        in_specs=(state, P(GRID, None, None)),
        out_specs=(state, state),
        check_vma=False,
    )
```

```python
import jax
import jax.numpy as jnp
from jax import lax
from jax.experimental import pallas as pl
from jax.experimental.pallas import tpu as pltpu
from jax.sharding import Mesh, PartitionSpec as P

FINE = 4
STEPS = 32
GROUP = 4

fine_along_z = (0.1, 0.12)
fine_along_x = (0.15, 0.12)
fine_along_y = (0.2, 0.12)
coarse_along_z = (0.2, 0.25)
coarse_along_x = (0.3, 0.25)
coarse_along_y = (0.4, 0.25)

AXES = ("z", "h", "c", "l", "y")
SLAB = ("z", "h", "c")
GRID = ("l", "y")
CORES = ("h", "l", "y")


def weights_of(kind):
    courant, diffuse = kind
    return diffuse + 0.5 * courant, 1.0 - 2.0 * diffuse, diffuse - 0.5 * courant


def line_filter(behind, middle, beyond, kind):
    a, b, c = weights_of(kind)
    return a * behind + b * middle + c * beyond


def side_weights(kind):
    a, b, c = weights_of(kind)
    return a / b, c / b


def scaled_filter(behind, middle, beyond, kind):
    a, c = side_weights(kind)
    return middle + (a * behind + c * beyond)


def even_lanes():
    return lax.broadcasted_iota(jnp.int32, (8, 128), 1) % 2 == 0


def packed_plane_filter(v, even):
    v = line_filter(pltpu.roll(v, 2, 1), v, pltpu.roll(v, 126, 1), coarse_along_y)
    right, left = pltpu.roll(v, 1, 1), pltpu.roll(v, 127, 1)
    behind = jnp.where(even, pltpu.roll(left, 1, 0), right)
    beyond = jnp.where(even, left, pltpu.roll(right, 7, 0))
    return line_filter(behind, v, beyond, coarse_along_x)


def packed_layer(ref, first, even):
    def rows(at):
        near = ref[pl.ds(first + at, 8, stride=4), :] + ref[pl.ds(first + at + 1, 8, stride=4), :]
        far = ref[pl.ds(first + 32 + at, 8, stride=4), :] + ref[pl.ds(first + 33 + at, 8, stride=4), :]
        return near + far

    low, high = rows(0), rows(2)
    return 0.125 * jnp.where(even, low + pltpu.roll(low, 127, 1), high + pltpu.roll(high, 1, 1))


def fine_kernel(one, two, from_one, from_two, ends, send_out, wide, all_rates, rates):
    even = even_lanes()
    is_first = (lax.axis_index("z") == 0) & (lax.axis_index("h") == 0) & (lax.axis_index("c") == 0)
    is_even = lax.axis_index("y") % 2 == 0
    wide[pl.ds(pl.multiple_of(jnp.where(is_even, 256, 0), 32), 128)] = from_one[96:224]
    wide[128:256] = one[96:224]
    wide[pl.ds(pl.multiple_of(jnp.where(is_even, 0, 256), 32), 128)] = from_two[0:128]
    rates[0:32] = jnp.where(is_even, two[128:160], one[0:32])
    rates[32:128] = jnp.where(is_even, one[0:96], two[128:224])
    all_rates[pl.ds(pl.multiple_of(jnp.where(is_even, 224, 0), 32), 96)] = from_one[0:96]
    all_rates[96:224] = rates[...]
    all_rates[pl.ds(pl.multiple_of(jnp.where(is_even, 0, 224), 32), 96)] = from_two[128:224]
    current = wide[...].reshape(12, 32, 128)
    rate = all_rates[...].reshape(10, 32, 128)
    middle = 1.0
    for kind in (fine_along_z, fine_along_x, fine_along_y):
        middle *= weights_of(kind)[1]
    drop, gain = 1.0 - rate, middle * rate
    for _ in range(FINE):
        mixed = scaled_filter(current[:-2], current[1:-1], current[2:], fine_along_z)
        mixed = scaled_filter(
            pltpu.roll(mixed, 1, 1), mixed, pltpu.roll(mixed, 31, 1), fine_along_x
        )
        mixed = scaled_filter(
            pltpu.roll(mixed, 1, 2), mixed, pltpu.roll(mixed, 127, 2), fine_along_y
        )
        current = drop * current[1:-1] + gain * mixed
        drop, gain = drop[1:-1], gain[1:-1]
    ends[...] = current.reshape(128, 128)
    coarse = [packed_layer(wide, 64 + 64 * i, even) for i in range(4)]
    flat = [packed_plane_filter(v, even) for v in coarse]
    coarse_rates, terms = [], []
    for i in range(2):
        coarse_rates.append(packed_layer(rates, 64 * i, even))
        mixed = line_filter(flat[i], flat[i + 1], flat[i + 2], coarse_along_z)
        guess = coarse[i + 1] + coarse_rates[i] * (mixed - coarse[i + 1])
        end = packed_layer(ends, 64 * i, even)
        terms.append(end - jnp.where(is_first, jnp.zeros_like(guess), guess))
    layer = jnp.where(lax.axis_index("h") == 0, coarse_rates[0], coarse_rates[1])
    layer = jnp.where(lax.axis_index("c") == 0, layer, pltpu.roll(layer, 4, 0))
    for i in range(2):
        for half in range(2):
            rows = terms[i][4 * half : 4 * half + 4]
            send_out[:, 2 * i + half] = jnp.broadcast_to(rows[None], (16, 4, 128))
    send_out[:, 4] = jnp.broadcast_to(layer[None, 0:4], (16, 4, 128))


def spread_pair(v, even):
    return jnp.where(even, v, pltpu.roll(v, 1, 1)), jnp.where(even, pltpu.roll(v, 127, 1), v)


def pair_filter(pair):
    low, high = (
        scaled_filter(pltpu.roll(v, 2, 1), v, pltpu.roll(v, 126, 1), coarse_along_y) for v in pair
    )
    return (
        scaled_filter(pltpu.roll(high, 1, 0), low, high, coarse_along_x),
        scaled_filter(low, high, pltpu.roll(low, 7, 0), coarse_along_x),
    )


def chain_kernel(received, from_core, send_out, history):
    even = even_lanes()
    is_first_core = lax.axis_index("c") == 0
    depth = range(16)
    part = lax.axis_index("l") * 4 + lax.axis_index("y")
    places = [lax.rem(part + i, 8) for i in range(8)]

    def piece(far, core, layer, row):
        first, second = (received, from_core) if core == 0 else (from_core, received)
        at = (8 * far + places[layer // 2], row)
        return jnp.where(is_first_core, first[at], second[at])

    middle = 1.0
    for kind in (coarse_along_z, coarse_along_x, coarse_along_y):
        middle *= weights_of(kind)[1]
    rates = [jnp.concatenate([piece(z % 2, core, z, 4) for core in range(2)], axis=0) for z in depth]
    rates = [spread_pair(rate, even) for rate in rates]
    drops = [[1.0 - rate for rate in pair] for pair in rates]
    rates = [[middle * rate for rate in pair] for pair in rates]

    def term(step):
        far, core = step // 2, step % 2
        rows = [[piece(far, core, z, 2 * (z % 2) + half) for half in range(2)] for z in depth]
        return [spread_pair(jnp.concatenate(halves, axis=0), even) for halves in rows]

    def keep(step, layers):
        for z in range(2):
            history[step, z] = jnp.where(even, *layers[z])

    def advance(layers, wanted):
        needed = range(wanted[0] - 1, wanted[-1] + 2) if len(wanted) < 16 else wanted
        flat = {z % 16: pair_filter(layers[z % 16]) for z in needed}
        out = [None] * 16
        for z in (z % 16 for z in wanted):
            behind, here, beyond = flat[(z - 1) % 16], flat[z], flat[(z + 1) % 16]
            mixed = [scaled_filter(*trio, coarse_along_z) for trio in zip(behind, here, beyond)]
            out[z] = [drops[z][i] * layers[z][i] + rates[z][i] * mixed[i] for i in range(2)]
        return out

    history[0] = jnp.zeros((2, 8, 128), jnp.float32)
    layers = term(0)
    keep(1, layers)
    for step in range(1, GROUP):
        later = advance(layers, depth)
        layers = [[a + b for a, b in zip(*both)] for both in zip(later, term(step))]
        keep(step + 1, layers)

    def body(step, layers):
        layers = advance(layers, depth)
        keep(step + 1, layers)
        return layers

    mine = lax.axis_index("z")
    stop = jnp.maximum(STEPS - GROUP * mine - GROUP, GROUP)
    layers = lax.fori_loop(GROUP, stop, body, layers)
    for i in range(GROUP):
        layers = advance(layers, range(i - GROUP + 1, GROUP + 1 - i))
        keep(stop + i + 1, layers)
    place = lax.axis_index("h") * 2 + lax.axis_index("c")
    for target in range(8):
        begin = jnp.where(mine <= target, GROUP * (target - mine) + place, 0)
        finish = jnp.where(mine <= target, GROUP * (target - mine) + place + 1, 0)
        if target == 0:
            begin = jnp.where(place == 0, STEPS - GROUP * mine, begin)
        send_out[target, 0:16] = history[begin].reshape(16, 128)
        send_out[target, 16:32] = history[finish].reshape(16, 128)


def add_spread(out, smooth, first, layer, even):
    low = jnp.where(even, layer, pltpu.roll(layer, 1, 1))
    high = jnp.where(even, pltpu.roll(layer, 127, 1), layer)
    for plane in (0, 32):
        for at, value in ((0, low), (1, low), (2, high), (3, high)):
            rows = pl.ds(first + plane + at, 8, stride=4)
            out[rows, :] = smooth[rows, :] + value


def finish_kernel(received, smooth, smooth_before, ends_out, starts_out):
    even = even_lanes()
    total = received[0]
    for source in range(1, 8):
        total = total + received[source]
    for i in range(2):
        before = total[8 * i : 8 * i + 8] - packed_layer(smooth_before, 64 * i, even)
        own = total[16 + 8 * i : 24 + 8 * i] - packed_layer(smooth, 64 * i, even)
        add_spread(starts_out, smooth_before, 64 * i, before, even)
        add_spread(ends_out, smooth, 64 * i, own, even)


def array(*shape):
    return jax.ShapeDtypeStruct(shape, jnp.float32)


def local(kernel, operands, outputs, buffers, operations, sent=True):
    if sent:
        outputs = jax.tree.map(lambda a: pltpu.VMEM(a.shape, a.dtype), outputs)
    return pl.pallas_call(
        kernel,
        out_shape=outputs,
        in_specs=[pl.BlockSpec(memory_space=pltpu.VMEM)] * len(operands),
        out_specs=jax.tree.map(lambda _: pl.BlockSpec(memory_space=pltpu.VMEM), outputs),
        scratch_shapes=buffers,
        cost_estimate=pl.CostEstimate(
            flops=operations, bytes_accessed=4 * sum(a.size for a in operands), transcendentals=0
        ),
        compiler_params=pltpu.CompilerParams(vmem_limit_bytes=16 * 2**20),
    )(*operands)


def scratch(*shape):
    return pltpu.VMEM(shape, jnp.float32)


def per_device(starts, cell_rates):
    start, rates = starts.reshape(128, 128), cell_rates.reshape(128, 128)
    is_even = lax.axis_index("y") % 2 == 0
    for_below, for_above = rates[:96], rates[32:]
    own = jnp.concatenate(
        [
            jnp.where(is_even, for_above, for_below),
            start,
            jnp.where(is_even, for_below, for_above),
        ],
        axis=0,
    )
    one, two = own[:224], own[96:]
    pairs = [(i, i ^ 1) for i in range(8)]
    others = [(i, (i - 1 + 2 * (i % 2)) % 8) for i in range(8)]
    from_one = lax.ppermute(one, GRID, pairs)
    from_two = lax.ppermute(two, GRID, others)
    smooth, message = local(
        fine_kernel,
        (one, two, from_one, from_two),
        (array(128, 128), array(16, 5, 4, 128)),
        [scratch(384, 128), scratch(320, 128), scratch(128, 128)],
        4_000_000,
    )
    gathered = lax.all_to_all(message, CORES, 0, 0, tiled=True)
    from_core = lax.ppermute(gathered, ("c",), [(0, 1), (1, 0)])
    pieces = local(
        chain_kernel,
        (gathered, from_core),
        array(8, 32, 128),
        [scratch(STEPS + 1, 2, 8, 128)],
        12_000_000,
    )
    pieces, smooth = lax.optimization_barrier((pieces, smooth))
    smooth_before = lax.ppermute(smooth, SLAB, [(i, (i + 1) % 32) for i in range(32)])
    shares = lax.all_to_all(pieces, ("z",), 0, 0, tiled=True)
    ends, nexts = local(
        finish_kernel,
        (shares, smooth, smooth_before),
        (array(128, 128), array(128, 128)),
        [],
        200_000,
        sent=False,
    )
    return ends.reshape(1, 4, 32, 128), nexts.reshape(1, 4, 32, 128)


def solution(mesh):
    fine_mesh = Mesh(mesh.devices.reshape(8, 2, 2, 2, 4), AXES)
    state = P(SLAB, GRID, None, None)
    return jax.shard_map(
        per_device,
        mesh=fine_mesh,
        in_specs=(state, P(GRID, None, None)),
        out_specs=(state, state),
        check_vma=False,
    )
```

```python
import jax
import jax.numpy as jnp
from jax import lax
from jax.experimental import pallas as pl
from jax.experimental.pallas import tpu as pltpu
from jax.sharding import Mesh, PartitionSpec as P

FINE = 4
STEPS = 32
GROUP = 4

fine_along_z = (0.1, 0.12)
fine_along_x = (0.15, 0.12)
fine_along_y = (0.2, 0.12)
coarse_along_z = (0.2, 0.25)
coarse_along_x = (0.3, 0.25)
coarse_along_y = (0.4, 0.25)

AXES = ("z", "h", "c", "l", "y")
SLAB = ("z", "h", "c")
GRID = ("l", "y")
CORES = ("h", "l", "y")


def weights_of(kind):
    courant, diffuse = kind
    return diffuse + 0.5 * courant, 1.0 - 2.0 * diffuse, diffuse - 0.5 * courant


def line_filter(behind, middle, beyond, kind):
    a, b, c = weights_of(kind)
    return a * behind + b * middle + c * beyond


def side_weights(kind):
    a, b, c = weights_of(kind)
    return a / b, c / b


def scaled_filter(behind, middle, beyond, kind):
    a, c = side_weights(kind)
    return middle + (a * behind + c * beyond)


def even_lanes():
    return lax.broadcasted_iota(jnp.int32, (8, 128), 1) % 2 == 0


def packed_plane_filter(v, even):
    v = line_filter(pltpu.roll(v, 2, 1), v, pltpu.roll(v, 126, 1), coarse_along_y)
    right, left = pltpu.roll(v, 1, 1), pltpu.roll(v, 127, 1)
    behind = jnp.where(even, pltpu.roll(left, 1, 0), right)
    beyond = jnp.where(even, left, pltpu.roll(right, 7, 0))
    return line_filter(behind, v, beyond, coarse_along_x)


def packed_layer(ref, first, even):
    def rows(at):
        near = ref[pl.ds(first + at, 8, stride=4), :] + ref[pl.ds(first + at + 1, 8, stride=4), :]
        far = ref[pl.ds(first + 32 + at, 8, stride=4), :] + ref[pl.ds(first + 33 + at, 8, stride=4), :]
        return near + far

    low, high = rows(0), rows(2)
    return 0.125 * jnp.where(even, low + pltpu.roll(low, 127, 1), high + pltpu.roll(high, 1, 1))


def fine_kernel(one, two, from_one, from_two, smooth_out, send_out, wide, ends, all_rates, rates):
    even = even_lanes()
    is_first = (lax.axis_index("z") == 0) & (lax.axis_index("h") == 0) & (lax.axis_index("c") == 0)
    is_even = lax.axis_index("y") % 2 == 0
    wide[pl.ds(pl.multiple_of(jnp.where(is_even, 256, 0), 32), 128)] = from_one[96:224]
    wide[128:256] = one[96:224]
    wide[pl.ds(pl.multiple_of(jnp.where(is_even, 0, 256), 32), 128)] = from_two[0:128]
    rates[0:32] = jnp.where(is_even, two[128:160], one[0:32])
    rates[32:128] = jnp.where(is_even, one[0:96], two[128:224])
    all_rates[pl.ds(pl.multiple_of(jnp.where(is_even, 224, 0), 32), 96)] = from_one[0:96]
    all_rates[96:224] = rates[...]
    all_rates[pl.ds(pl.multiple_of(jnp.where(is_even, 0, 224), 32), 96)] = from_two[128:224]
    current = wide[...].reshape(12, 32, 128)
    rate = all_rates[...].reshape(10, 32, 128)
    middle = 1.0
    for kind in (fine_along_z, fine_along_x, fine_along_y):
        middle *= weights_of(kind)[1]
    drop, gain = 1.0 - rate, middle * rate
    for _ in range(FINE):
        mixed = scaled_filter(current[:-2], current[1:-1], current[2:], fine_along_z)
        mixed = scaled_filter(
            pltpu.roll(mixed, 1, 1), mixed, pltpu.roll(mixed, 31, 1), fine_along_x
        )
        mixed = scaled_filter(
            pltpu.roll(mixed, 1, 2), mixed, pltpu.roll(mixed, 127, 2), fine_along_y
        )
        current = drop * current[1:-1] + gain * mixed
        drop, gain = drop[1:-1], gain[1:-1]
    ends[...] = current.reshape(128, 128)
    coarse = [packed_layer(wide, 64 + 64 * i, even) for i in range(4)]
    flat = [packed_plane_filter(v, even) for v in coarse]
    coarse_rates, terms = [], []
    for i in range(2):
        coarse_rates.append(packed_layer(rates, 64 * i, even))
        mixed = line_filter(flat[i], flat[i + 1], flat[i + 2], coarse_along_z)
        guess = coarse[i + 1] + coarse_rates[i] * (mixed - coarse[i + 1])
        end = packed_layer(ends, 64 * i, even)
        terms.append(end - jnp.where(is_first, jnp.zeros_like(guess), guess))
        add_spread(smooth_out, ends, 64 * i, -end, even)
    layer = jnp.where(lax.axis_index("h") == 0, coarse_rates[0], coarse_rates[1])
    layer = jnp.where(lax.axis_index("c") == 0, layer, pltpu.roll(layer, 4, 0))
    for i in range(2):
        for half in range(2):
            rows = terms[i][4 * half : 4 * half + 4]
            send_out[:, 2 * i + half] = jnp.broadcast_to(rows[None], (16, 4, 128))
    send_out[:, 4] = jnp.broadcast_to(layer[None, 0:4], (16, 4, 128))


def spread_pair(v, even):
    return jnp.where(even, v, pltpu.roll(v, 1, 1)), jnp.where(even, pltpu.roll(v, 127, 1), v)


def pair_filter(pair):
    low, high = (
        scaled_filter(pltpu.roll(v, 2, 1), v, pltpu.roll(v, 126, 1), coarse_along_y) for v in pair
    )
    return (
        scaled_filter(pltpu.roll(high, 1, 0), low, high, coarse_along_x),
        scaled_filter(low, high, pltpu.roll(low, 7, 0), coarse_along_x),
    )


def chain_kernel(received, from_core, send_out, history):
    even = even_lanes()
    is_first_core = lax.axis_index("c") == 0
    depth = range(16)
    part = lax.axis_index("l") * 4 + lax.axis_index("y")
    places = [lax.rem(part + i, 8) for i in range(8)]

    def piece(far, core, layer, row):
        first, second = (received, from_core) if core == 0 else (from_core, received)
        at = (8 * far + places[layer // 2], row)
        return jnp.where(is_first_core, first[at], second[at])

    middle = 1.0
    for kind in (coarse_along_z, coarse_along_x, coarse_along_y):
        middle *= weights_of(kind)[1]
    rates = [jnp.concatenate([piece(z % 2, core, z, 4) for core in range(2)], axis=0) for z in depth]
    rates = [spread_pair(rate, even) for rate in rates]

    def term(step):
        far, core = step // 2, step % 2
        rows = [[piece(far, core, z, 2 * (z % 2) + half) for half in range(2)] for z in depth]
        return [spread_pair(jnp.concatenate(halves, axis=0), even) for halves in rows]

    def keep(step, layers):
        for z in range(2):
            history[step, z] = jnp.where(even, *layers[z])

    def advance(layers, wanted):
        needed = range(wanted[0] - 1, wanted[-1] + 2) if len(wanted) < 16 else wanted
        flat = {z % 16: pair_filter(layers[z % 16]) for z in needed}
        out = [None] * 16
        for z in (z % 16 for z in wanted):
            behind, here, beyond = flat[(z - 1) % 16], flat[z], flat[(z + 1) % 16]
            mixed = [scaled_filter(*trio, coarse_along_z) for trio in zip(behind, here, beyond)]
            out[z] = [
                layers[z][i] + rates[z][i] * (middle * mixed[i] - layers[z][i]) for i in range(2)
            ]
        return out

    history[0] = jnp.zeros((2, 8, 128), jnp.float32)
    layers = term(0)
    keep(1, layers)
    for step in range(1, GROUP):
        later = advance(layers, depth)
        layers = [[a + b for a, b in zip(*both)] for both in zip(later, term(step))]
        keep(step + 1, layers)

    def body(turn, layers):
        for step in (GROUP + 2 * turn, GROUP + 2 * turn + 1):
            layers = advance(layers, depth)
            keep(step + 1, layers)
        return layers

    mine = lax.axis_index("z")
    stop = jnp.maximum(STEPS - GROUP * mine - GROUP, GROUP)
    layers = lax.fori_loop(0, (stop - GROUP) // 2, body, layers)
    for i in range(GROUP):
        layers = advance(layers, range(i - GROUP + 1, GROUP + 1 - i))
        keep(stop + i + 1, layers)
    place = lax.axis_index("h") * 2 + lax.axis_index("c")
    for target in range(8):
        begin = jnp.where(mine <= target, GROUP * (target - mine) + place, 0)
        finish = jnp.where(mine <= target, GROUP * (target - mine) + place + 1, 0)
        if target == 0:
            begin = jnp.where(place == 0, STEPS - GROUP * mine, begin)
        send_out[target, 0:16] = history[begin].reshape(16, 128)
        send_out[target, 16:32] = history[finish].reshape(16, 128)


def add_spread(out, smooth, first, layer, even):
    low = jnp.where(even, layer, pltpu.roll(layer, 1, 1))
    high = jnp.where(even, pltpu.roll(layer, 127, 1), layer)
    for plane in (0, 32):
        for at, value in ((0, low), (1, low), (2, high), (3, high)):
            rows = pl.ds(first + plane + at, 8, stride=4)
            out[rows, :] = smooth[rows, :] + value


def finish_kernel(received, smooth, smooth_before, ends_out, starts_out):
    even = even_lanes()
    total = received[0]
    for source in range(1, 8):
        total = total + received[source]
    for i in range(2):
        add_spread(starts_out, smooth_before, 64 * i, total[8 * i : 8 * i + 8], even)
        add_spread(ends_out, smooth, 64 * i, total[16 + 8 * i : 24 + 8 * i], even)


def array(*shape):
    return jax.ShapeDtypeStruct(shape, jnp.float32)


def local(kernel, operands, outputs, buffers, operations, sent=True):
    if sent:
        outputs = jax.tree.map(lambda a: pltpu.VMEM(a.shape, a.dtype), outputs)
    return pl.pallas_call(
        kernel,
        out_shape=outputs,
        in_specs=[pl.BlockSpec(memory_space=pltpu.VMEM)] * len(operands),
        out_specs=jax.tree.map(lambda _: pl.BlockSpec(memory_space=pltpu.VMEM), outputs),
        scratch_shapes=buffers,
        cost_estimate=pl.CostEstimate(
            flops=operations, bytes_accessed=4 * sum(a.size for a in operands), transcendentals=0
        ),
        compiler_params=pltpu.CompilerParams(vmem_limit_bytes=16 * 2**20),
    )(*operands)


def scratch(*shape):
    return pltpu.VMEM(shape, jnp.float32)


def per_device(starts, cell_rates):
    start, rates = starts.reshape(128, 128), cell_rates.reshape(128, 128)
    is_even = lax.axis_index("y") % 2 == 0
    for_below, for_above = rates[:96], rates[32:]
    own = jnp.concatenate(
        [
            jnp.where(is_even, for_above, for_below),
            start,
            jnp.where(is_even, for_below, for_above),
        ],
        axis=0,
    )
    one, two = own[:224], own[96:]
    pairs = [(i, i ^ 1) for i in range(8)]
    others = [(i, (i - 1 + 2 * (i % 2)) % 8) for i in range(8)]
    from_one = lax.ppermute(one, GRID, pairs)
    from_two = lax.ppermute(two, GRID, others)
    smooth, message = local(
        fine_kernel,
        (one, two, from_one, from_two),
        (array(128, 128), array(16, 5, 4, 128)),
        [scratch(384, 128), scratch(128, 128), scratch(320, 128), scratch(128, 128)],
        4_000_000,
    )
    gathered = lax.all_to_all(message, CORES, 0, 0, tiled=True)
    from_core = lax.ppermute(gathered, ("c",), [(0, 1), (1, 0)])
    pieces = local(
        chain_kernel,
        (gathered, from_core),
        array(8, 32, 128),
        [scratch(STEPS + 1, 2, 8, 128)],
        12_000_000,
    )
    pieces, smooth = lax.optimization_barrier((pieces, smooth))
    smooth_before = lax.ppermute(smooth, SLAB, [(i, (i + 1) % 32) for i in range(32)])
    shares = lax.all_to_all(pieces, ("z",), 0, 0, tiled=True)
    ends, nexts = local(
        finish_kernel,
        (shares, smooth, smooth_before),
        (array(128, 128), array(128, 128)),
        [],
        200_000,
        sent=False,
    )
    return ends.reshape(1, 4, 32, 128), nexts.reshape(1, 4, 32, 128)


def solution(mesh):
    fine_mesh = Mesh(mesh.devices.reshape(8, 2, 2, 2, 4), AXES)
    state = P(SLAB, GRID, None, None)
    return jax.shard_map(
        per_device,
        mesh=fine_mesh,
        in_specs=(state, P(GRID, None, None)),
        out_specs=(state, state),
        check_vma=False,
    )
```
